32 devices in a mesh: corridor: 8 (over z, x), group: 4 (over y, core).
Axes of the slice: x: 2, y: 2, z: 4, core: 2. Of those that a mesh axis runs over, the one named last changes fastest.
Arguments:
- features: bfloat16 [384, 64, 512], P(('corridor', 'group')), may hold values from -6 to 6
- voxel_mask: int32 [384, 512], P(('corridor', 'group')), may hold values from 0 to 1, as said below
- neighbours: int32 [384, 26], P(('corridor', 'group')), may hold values from -1 to 383, as said below
- weight_first: bfloat16 [27, 64, 64], replicated, may hold values from -0.15625 to 0.15625
- gain_first: float32 [64], replicated, may hold values from 0.25 to 1.75
- offset_first: float32 [64], replicated, may hold values from -3 to 3
- weight_second: bfloat16 [27, 128, 64], replicated, may hold values from -0.15625 to 0.15625
- gain_second: float32 [128], replicated, may hold values from 0.25 to 1.75
- offset_second: float32 [128], replicated, may hold values from -3 to 3
Outputs:
- segment_features: bfloat16 [384, 128, 512], P(('corridor', 'group'))
The draws below stay inside these ranges and needn't reach their ends.
Inputs may be any that keep to these rules, and one draw needn't show every extreme that they name: `neighbours`: global slot of a device's slot s is (corridor index * 4 + group index) * 12 + s. Entry d names the brick displaced by the d-th of the 26 nonzero triples (dx slowest, lexicographic); its owner's corridor index differs by at most one from the brick's own, and differs only where dx is nonzero, by dx. Adjacency is symmetric. Empty slots have an all-zero mask and only -1 entries, and no entry names them. `voxel_mask`: every occupied brick is a slot named by the adjacency of its neighbours.
All inputs are finite; a program needn't handle non-finite values.
Results may differ from the reference program's by a relative error of at most 0.0051.
Values may be sent and summed in bfloat16 or wider, within the bound.
A program may use at most 320 MiB of HBM per device.

```python
import jax
import jax.numpy as jnp
from jax import lax

C = 64
C2 = 128
BRICK = 8
SECTION_LEN = 4
BRICK_DEV = 12
SECTIONS = 8
LANES = 4
BRICKS = 384


DIRECTIONS = [(a, b, c) for a in (-1, 0, 1) for b in (-1, 0, 1) for c in (-1, 0, 1) if (a, b, c) != (0, 0, 0)]


def build_world(key):
    base = jax.random.fold_in(key, 7)
    key_occ, key_perm, key_level, key_voxel = jax.random.split(base, 4)
    width_y = LANES
    width_z = BRICK_DEV // 4
    per_section = LANES * BRICK_DEV
    sections = jnp.arange(SECTIONS, dtype=jnp.int32)
    limit = 30 + 60 * sections // max(SECTIONS - 1, 1)
    occupied = jax.random.randint(key_occ, (SECTIONS, per_section), 0, 100) < limit[:, None]
    perms = jax.vmap(lambda k: jax.random.permutation(k, per_section))(jax.random.split(key_perm, SECTIONS)).astype(jnp.int32)
    inverse = jnp.zeros((SECTIONS, per_section), jnp.int32).at[sections[:, None], perms].set(jnp.arange(per_section, dtype=jnp.int32)[None, :])
    cx = perms // (width_y * width_z)
    cy = perms // width_z % width_y
    cz = perms % width_z
    slot_occ = jnp.take_along_axis(occupied, perms, axis=1)
    columns = []
    for step in DIRECTIONS:
        gx = sections[:, None] * SECTION_LEN + cx + step[0]
        other = jnp.floor_divide(gx, SECTION_LEN)
        lx = gx - other * SECTION_LEN
        ly = cy + step[1]
        lz = cz + step[2]
        inside = (other >= 0) & (other < SECTIONS) & (ly >= 0) & (ly < width_y) & (lz >= 0) & (lz < width_z)
        other_c = jnp.clip(other, 0, SECTIONS - 1)
        cand = jnp.clip(lx * width_y * width_z + jnp.clip(ly, 0, width_y - 1) * width_z + jnp.clip(lz, 0, width_z - 1), 0, per_section - 1)
        live = inside & occupied[other_c, cand] & slot_occ
        ident = other_c * per_section + inverse[other_c, cand]
        columns.append(jnp.where(live, ident, -1))
    nbrs = jnp.stack(columns, axis=-1).reshape(BRICKS, 26).astype(jnp.int32)
    level = jax.random.randint(key_level, (SECTIONS, per_section, 1), 30, 95)
    voxels = (jax.random.randint(key_voxel, (SECTIONS, per_section, BRICK ** 3), 0, 100) < level) & slot_occ[:, :, None]
    return (nbrs, voxels.astype(jnp.int32).reshape(BRICKS, BRICK ** 3))


def draw_neighbours(key, part):
    return build_world(key)[0]


def draw_voxel_mask(key, part):
    return build_world(key)[1]


def draw_features(key, part):
    inner = jax.random.fold_in(key, 11)
    values = jax.random.normal(inner, (BRICKS, C, BRICK ** 3), jnp.float32)
    return jnp.clip(values, -6.0, 6.0).astype(jnp.bfloat16)


def scatter_about(stream_key, dims, scale, most, kind=jnp.bfloat16):
    array = jax.random.normal(stream_key, dims, jnp.float32) * scale
    return jnp.minimum(jnp.maximum(array, -most), most).astype(kind)


def setup_inputs(seed: int = 0) -> dict:
    splits = jax.random.split(jax.random.key(seed), 10)
    features = draw_features(jax.random.fold_in(splits[9], 71), 0)
    voxel_mask = draw_voxel_mask(jax.random.fold_in(splits[9], 71), 0)
    neighbours = draw_neighbours(jax.random.fold_in(splits[9], 71), 0)
    weight_first = scatter_about(splits[3], (27, C, C), (27 * C) ** -0.5, 0.15625)
    gain_first = jnp.clip(1.0 + 0.15 * jax.random.normal(splits[4], (C,), jnp.float32), 0.25, 1.75)
    offset_first = scatter_about(splits[5], (C,), 0.5, 3.0, jnp.float32)
    weight_second = scatter_about(splits[6], (27, C2, C), (27 * C) ** -0.5, 0.15625)
    gain_second = jnp.clip(1.0 + 0.15 * jax.random.normal(splits[7], (C2,), jnp.float32), 0.25, 1.75)
    offset_second = scatter_about(splits[8], (C2,), 0.5, 3.0, jnp.float32)
    return dict(features=features, voxel_mask=voxel_mask, neighbours=neighbours, weight_first=weight_first, gain_first=gain_first, offset_first=offset_first, weight_second=weight_second, gain_second=gain_second, offset_second=offset_second)


DIRECTIONS = [(a, b, c) for a in (-1, 0, 1) for b in (-1, 0, 1) for c in (-1, 0, 1) if (a, b, c) != (0, 0, 0)]

def cell_range(step):
    if step < 0:
        return (7, 8, 0)
    if step == 0:
        return (0, 8, 1)
    return (0, 1, 9)

def conv_layer(field, mask_f, neighbours, weight):
    total_rows, chans = (field.shape[0], field.shape[1])
    outs = weight.shape[1]
    cubes = field.reshape(total_rows, chans, 8, 8, 8)
    blocks = total_rows // BRICK_DEV

    def one_block(index):
        start = (index * BRICK_DEV).astype(jnp.int32)
        own = lax.dynamic_slice_in_dim(cubes, start, BRICK_DEV, 0)
        ids = lax.dynamic_slice_in_dim(neighbours, start, BRICK_DEV, 0)
        masks = lax.dynamic_slice_in_dim(mask_f, start, BRICK_DEV, 0)
        padded = jnp.zeros((BRICK_DEV, chans, 10, 10, 10), jnp.bfloat16)
        padded = padded.at[:, :, 1:9, 1:9, 1:9].set(own)
        for idx, step in enumerate(DIRECTIONS):
            column = ids[:, idx]
            nbr = jnp.take(cubes, jnp.maximum(column, 0).astype(jnp.int32), axis=0)
            nbr = jnp.where((column >= 0)[:, None, None, None, None], nbr, jnp.zeros((), jnp.bfloat16))
            rx, ry, rz = (cell_range(step[0]), cell_range(step[1]), cell_range(step[2]))
            piece = nbr[:, :, rx[0]:rx[1], ry[0]:ry[1], rz[0]:rz[1]]
            padded = padded.at[:, :, rx[2]:rx[2] + rx[1] - rx[0], ry[2]:ry[2] + ry[1] - ry[0], rz[2]:rz[2] + rz[1] - rz[0]].set(piece)
        padded_f = padded.astype(jnp.float32)
        total = jnp.zeros((BRICK_DEV, outs, 8, 8, 8), jnp.float32)
        for tap in range(27):
            oa, oe, of_ = (tap // 9, tap // 3 % 3, tap % 3)
            total = total + jnp.einsum('oc,bcxyz->boxyz', weight[tap].astype(jnp.float32), padded_f[:, :, oa:oa + 8, oe:oe + 8, of_:of_ + 8])
        return total.reshape(BRICK_DEV, outs, 512) * masks[:, None, :]
    values = lax.map(one_block, jnp.arange(blocks))
    return values.reshape(total_rows, outs, 512)

def normalize(values, mask_f, count, gain, offset):
    mean = lax.optimization_barrier(jnp.sum(values, axis=(0, 2))) / count
    deviation = values - mean[None, :, None]
    var = lax.optimization_barrier(jnp.sum(mask_f[:, None, :] * deviation * deviation, axis=(0, 2))) / count
    scaled = gain[None, :, None] * deviation / jnp.sqrt(var[None, :, None] + 1e-05) + offset[None, :, None]
    return (jnp.maximum(scaled, 0.0) * mask_f[:, None, :]).astype(jnp.bfloat16)

def reference(features, voxel_mask, neighbours, weight_first, gain_first, offset_first, weight_second, gain_second, offset_second):
    mask_f = voxel_mask.astype(jnp.float32)
    masked = features * voxel_mask.astype(jnp.bfloat16)[:, None, :]
    count = jnp.sum(mask_f)
    first = conv_layer(masked, mask_f, neighbours, weight_first)
    hidden = normalize(first, mask_f, count, gain_first, offset_first)
    second = conv_layer(hidden, mask_f, neighbours, weight_second)
    return normalize(second, mask_f, count, gain_second, offset_second)
```

```python
import functools

import jax
import jax.numpy as jnp
from jax import lax
from jax.experimental import pallas as pl
from jax.experimental.pallas import tpu as pltpu
from jax.sharding import PartitionSpec as P

DIRECTIONS = [
    (a, b, c) for a in (-1, 0, 1) for b in (-1, 0, 1) for c in (-1, 0, 1) if (a, b, c) != (0, 0, 0)
]
AT = {step: idx for idx, step in enumerate(DIRECTIONS)}
SOURCES = ((0, 1, 2, 3, 4, 5, 8, -1), (2, 3, 4, 5, 8, -1, 6, 7))
F32 = jnp.float32
BF16 = jnp.bfloat16
VMEM = pl.BlockSpec(memory_space=pltpu.VMEM)
SMEM = pl.BlockSpec(memory_space=pltpu.SMEM)
MESH = pl.DeviceIdType.MESH


def params(mib, **kw):
    return pltpu.CompilerParams(vmem_limit_bytes=mib * 1024 * 1024, **kw)


def spread(mask_rows, width):
    shift = {64: 6, 128: 7}[width]
    row = lax.broadcasted_iota(jnp.int32, (128, 8 * width), 0)
    lane = lax.broadcasted_iota(jnp.int32, (128, 8 * width), 1)
    pick = jnp.where((lane >> shift) == row, 1.0, 0.0).astype(BF16)
    return jnp.dot(mask_rows, pick, preferred_element_type=F32)


def emit_field(nb, tiles, field_ref, bundle_ref, z_ref):
    face = nb * 8
    for t in range(4):
        value = tiles[t]
        cols = slice(128 * t, 128 * t + 128)
        field_ref[:, cols] = value[...].astype(BF16)
        bundle_ref[0:face, cols] = value[0:face, :].astype(BF16)
        bundle_ref[face : 2 * face, cols] = value[7 * face : 8 * face, :].astype(BF16)
        bundle_ref[2 * face : 3 * face, cols] = value[pl.ds(0, face, stride=8), :].astype(BF16)
        bundle_ref[3 * face : 4 * face, cols] = value[pl.ds(7, face, stride=8), :].astype(BF16)
    lane = lax.broadcasted_iota(jnp.int32, (8 * face, 128), 1)
    z_ref[...] = jnp.where(lane < 64, tiles[0][...], tiles[3][...]).astype(BF16)


def field_shapes(nb):
    return (
        jax.ShapeDtypeStruct((nb * 64, 512), BF16),
        jax.ShapeDtypeStruct((nb * 32, 512), BF16),
        jax.ShapeDtypeStruct((nb * 64, 128), BF16),
    )


def prepare_kernel(nb, x_ref, m_ref, field_ref, bundle_ref, z_ref, t_ref, *tiles):
    lane = lax.broadcasted_iota(jnp.int32, (64, 128), 1)
    for pair in range(nb // 2):
        halves = [
            x_ref[2 * pair + k].astype(F32) * m_ref[pl.ds(2 * pair + k, 1), :] for k in range(2)
        ]
        t_ref[...] = jnp.concatenate(halves, axis=0).T
        for t in range(4):
            even = t_ref[pl.ds(2 * t, 64, stride=8), :]
            odd = t_ref[pl.ds(2 * t + 1, 64, stride=8), :]
            first = jnp.where(lane < 64, even, pltpu.roll(odd, 64, 1))
            second = jnp.where(lane < 64, pltpu.roll(even, 64, 1), odd)
            for x in range(8):
                base = x * nb * 8 + pair * 16
                tiles[t][base : base + 8, :] = first[8 * x : 8 * x + 8]
                tiles[t][base + 8 : base + 16, :] = second[8 * x : 8 * x + 8]
    emit_field(nb, tiles, field_ref, bundle_ref, z_ref)


def prepare(features, mask_f):
    nb = features.shape[0]
    return pl.pallas_call(
        functools.partial(prepare_kernel, nb),
        out_shape=field_shapes(nb),
        in_specs=[VMEM, VMEM],
        out_specs=(VMEM, VMEM, VMEM),
        scratch_shapes=[pltpu.VMEM((512, 128), F32)]
        + [pltpu.VMEM((nb * 64, 128), F32) for _ in range(4)],
        compiler_params=params(32),
    )(features, mask_f)


def conv_kernel(
    nb, lanes, outs, rows_ref, field_ref, pool_ref, zpool_ref, w_ref, m_ref,
    out_ref, stat_ref, own_ref, pf_ref, zf_ref, q_ref, wb_ref,
):
    face = nb * 8
    total = pool_ref.shape[0]
    ztotal = zpool_ref.shape[0]
    own_ref[...] = field_ref[...].astype(F32)
    pf_ref[0:total, :] = pool_ref[...].astype(F32)
    pf_ref[total:, :] = jnp.zeros((face, 512), F32)
    zf_ref[0:ztotal, :] = zpool_ref[...].astype(F32)
    zf_ref[ztotal:, :] = jnp.zeros((8 * face, 128), F32)

    wb_ref[...] = jnp.zeros(wb_ref.shape, BF16)
    for half in range(2):
        for a in range(3):
            for e in range(3):
                for at, source in enumerate(SOURCES[half]):
                    row = e * 512 + at * 64
                    for q in range(outs * 4 // 128):
                        z = 4 * half + q * 128 // outs
                        f = source - z + 1
                        kinds = 3 if outs == 128 else 4
                        if 0 <= f < kinds:
                            block = ((a * 3 + e) * kinds + f) * 64
                            wb_ref[half, a, row : row + 64, q * 128 : q * 128 + 128] = w_ref[
                                block : block + 64, :
                            ]

    low = lax.broadcasted_iota(jnp.int32, (8, 128), 1) < 64
    sub = lax.broadcasted_iota(jnp.int32, (8, 128), 0)

    def brick_planes(b):
        def at(dx, dy, dz):
            return rows_ref[b, AT[(dx, dy, dz)]]

        def faces(load):
            main = load(0)
            up = load(1)
            down = load(-1)
            tiles = [main[:, 128 * t : 128 * t + 128] for t in range(4)]
            width = main.shape[0]
            halo = jnp.where(low[:width], up[:, 0:128], down[:, 384:512])
            return [tiles[0], tiles[1], tiles[2], halo, tiles[3]]

        def x_face(dx, dy):
            def load(dz):
                return pf_ref[pl.ds(pl.multiple_of(at(dx, dy, dz), 8), 8), :]

            return faces(load)

        def y_row(dy, x):
            def load(dz):
                return pf_ref[pl.ds(at(0, dy, dz) + x * nb, 1), :]

            return [jnp.broadcast_to(v, (8, 128)) for v in faces(load)]

        def inner(x):
            base = pl.multiple_of(x * face + b * 8, 8)
            own = own_ref[pl.ds(base, 8), :]
            up = zf_ref[pl.ds(pl.multiple_of(at(0, 0, 1) + x * face, 8), 8), :]
            down = zf_ref[pl.ds(pl.multiple_of(at(0, 0, -1) + x * face, 8), 8), :]
            tiles = [own[:, 128 * t : 128 * t + 128] for t in range(4)]
            return [tiles[0], tiles[1], tiles[2], jnp.where(low, up, down), tiles[3]]

        planes = []
        for i in range(10):
            if i == 0 or i == 9:
                dx = -1 if i == 0 else 1
                centre = x_face(dx, 0)
                before = x_face(dx, -1)
                after = x_face(dx, 1)
            else:
                centre = inner(i - 1)
                before = y_row(-1, i - 1)
                after = y_row(1, i - 1)
            shifted0 = [
                pltpu.roll(jnp.where(sub == 7, n, c), 1, 0) for n, c in zip(before, centre)
            ]
            shifted2 = [
                pltpu.roll(jnp.where(sub == 0, n, c), 7, 0) for n, c in zip(after, centre)
            ]
            planes.append((shifted0, centre, shifted2))
        return planes

    @pl.loop(0, nb // 2)
    def _(pair):
        first = brick_planes(2 * pair)
        second = brick_planes(2 * pair + 1)
        for i in range(10):
            rows = pl.ds(pl.multiple_of(i * face + pair * 16, 16), 16)
            for e in range(3):
                tiles = [
                    jnp.concatenate([u, v], axis=0).astype(BF16)
                    for u, v in zip(first[i][e], second[i][e])
                ]
                for t in range(4):
                    q_ref[0, rows, e * 512 + t * 128 : e * 512 + t * 128 + 128] = tiles[t]
                    q_ref[1, rows, e * 512 + t * 128 : e * 512 + t * 128 + 128] = tiles[t + 1]

    mask_rows = m_ref[...]
    mask = spread(mask_rows, outs)
    sums = jnp.zeros((1, 128), F32)
    for half in range(2):
        acc = None
        for a in range(3):
            part = jnp.dot(
                q_ref[half, a * face : a * face + 8 * face, :],
                wb_ref[half, a],
                preferred_element_type=F32,
            )
            acc = part if acc is None else acc + part
        span = slice(half * 4 * outs, half * 4 * outs + 4 * outs)
        acc = acc * mask[:, span]
        out_ref[:, span] = acc
        column = jnp.sum(acc, axis=0, keepdims=True)
        for t in range(4 * outs // 128):
            sums = sums + column[:, 128 * t : 128 * t + 128]
    if outs == 64:
        sums = sums + pltpu.roll(sums, 64, 1)
    count = jnp.sum(mask_rows.astype(F32))
    mean = sums / jnp.maximum(count, 1.0)
    squares = jnp.zeros((1, 128), F32)
    for t in range(8 * outs // 128):
        span = slice(128 * t, 128 * t + 128)
        deviation = (out_ref[:, span] - mean) * mask[:, span]
        squares = squares + jnp.sum(deviation * deviation, axis=0, keepdims=True)
    if outs == 64:
        squares = squares + pltpu.roll(squares, 64, 1)
    stat_ref[...] = jnp.zeros((8, 128), F32)
    stat_ref[0:1, :] = sums
    stat_ref[1:2, :] = squares
    stat_ref[2:3, :] = jnp.full((1, 128), count, F32)


def conv(rows, field, pool, zpool, weight, mask_rows, lanes, outs):
    nb = rows.shape[0]
    return pl.pallas_call(
        functools.partial(conv_kernel, nb, lanes, outs),
        out_shape=(
            jax.ShapeDtypeStruct((nb * 64, 8 * outs), F32),
            jax.ShapeDtypeStruct((8, 128), F32),
        ),
        in_specs=[SMEM, VMEM, VMEM, VMEM, VMEM, VMEM],
        out_specs=(VMEM, VMEM),
        scratch_shapes=[
            pltpu.VMEM((nb * 64, 512), F32),
            pltpu.VMEM((pool.shape[0] + nb * 8, 512), F32),
            pltpu.VMEM((zpool.shape[0] + nb * 64, 128), F32),
            pltpu.VMEM((2, nb * 80, 1536), BF16),
            pltpu.VMEM((2, 3, 1536, 4 * outs), BF16),
        ],
        compiler_params=params(58),
    )(rows, field, pool, zpool, weight, mask_rows)


def merge(parts):
    sums = jnp.sum(parts[:, 0:1, :], axis=0)
    counts = jnp.sum(parts[:, 2:3, :], axis=0)
    mean = sums / jnp.maximum(counts, 1.0)
    gaps = parts[:, 0:1, :] / jnp.maximum(parts[:, 2:3, :], 1.0) - mean[None]
    squares = jnp.sum(parts[:, 1:2, :] + parts[:, 2:3, :] * gaps * gaps, axis=0)
    return sums, squares, counts


def stats_kernel(sections, lanes, stat_ref, out_ref, near, far, mid, send, recv, send2, recv2):
    s = lax.axis_index("corridor")
    g = lax.axis_index("group")
    barrier = pltpu.get_barrier_semaphore()

    def lane_peer(d):
        return (s, lax.rem(g + d, lanes))

    def section_peer(d):
        return (lax.rem(s + d, sections), g)

    @pl.loop(1, lanes)
    def _(d):
        pl.semaphore_signal(barrier, inc=1, device_id=lane_peer(d), device_id_type=MESH)

    @pl.loop(1, sections)
    def _(d):
        pl.semaphore_signal(barrier, inc=1, device_id=section_peer(d), device_id_type=MESH)

    pl.semaphore_wait(barrier, lanes + sections - 2)

    def exchange(src, dst, me, count, peer, send_sem, recv_sem):
        def copy(d, slot):
            return pltpu.make_async_remote_copy(
                src_ref=src, dst_ref=dst.at[slot], send_sem=send_sem.at[d],
                recv_sem=recv_sem.at[slot], device_id=peer(d), device_id_type=MESH,
            )

        @pl.loop(1, count)
        def _(d):
            copy(d, me).start()

        dst[me] = src[...]

        @pl.loop(1, count)
        def _(d):
            copy(d, lax.rem(me + count - d, count)).wait_recv()

        @pl.loop(1, count)
        def _(d):
            copy(d, me).wait_send()

    exchange(stat_ref, near, g, lanes, lane_peer, send, recv)
    sums, squares, counts = merge(near[...])
    mid[...] = jnp.zeros((8, 128), F32)
    mid[0:1, :] = sums
    mid[1:2, :] = squares
    mid[2:3, :] = counts
    exchange(mid, far, s, sections, section_peer, send2, recv2)
    sums, squares, counts = merge(far[...])
    out_ref[...] = jnp.zeros((8, 128), F32)
    out_ref[0:1, :] = sums / counts
    out_ref[1:2, :] = squares / counts


def global_stats(stat, collective):
    sections = lax.axis_size("corridor")
    lanes = lax.axis_size("group")
    return pl.pallas_call(
        functools.partial(stats_kernel, sections, lanes),
        out_shape=jax.ShapeDtypeStruct((8, 128), F32),
        in_specs=[VMEM],
        out_specs=VMEM,
        scratch_shapes=[
            pltpu.VMEM((lanes, 8, 128), F32),
            pltpu.VMEM((sections, 8, 128), F32),
            pltpu.VMEM((8, 128), F32),
            pltpu.SemaphoreType.DMA((lanes,)),
            pltpu.SemaphoreType.DMA((lanes,)),
            pltpu.SemaphoreType.DMA((sections,)),
            pltpu.SemaphoreType.DMA((sections,)),
        ],
        compiler_params=params(16, collective_id=collective, has_side_effects=True),
    )(stat)


def scaled(value, stat_ref, gain_ref, offset_ref):
    mean = stat_ref[0:1, :]
    deviation = value - mean
    root = jnp.sqrt(stat_ref[1:2, :] + 1e-05)
    return jnp.maximum(gain_ref[...] * deviation / root + offset_ref[...], 0.0)


def hidden_kernel(
    nb, v_ref, stat_ref, gain_ref, offset_ref, m_ref, field_ref, bundle_ref, z_ref, *tiles
):
    mask = spread(m_ref[...], 64)
    for t in range(4):
        span = slice(128 * t, 128 * t + 128)
        tiles[t][...] = scaled(v_ref[:, span], stat_ref, gain_ref, offset_ref) * mask[:, span]
    emit_field(nb, tiles, field_ref, bundle_ref, z_ref)


def make_hidden(first, stat, gain, offset, mask_rows):
    nb = first.shape[0] // 64
    return pl.pallas_call(
        functools.partial(hidden_kernel, nb),
        out_shape=field_shapes(nb),
        in_specs=[VMEM] * 5,
        out_specs=(VMEM, VMEM, VMEM),
        scratch_shapes=[pltpu.VMEM((nb * 64, 128), F32) for _ in range(4)],
        compiler_params=params(32),
    )(first, stat, gain, offset, mask_rows)


def final_kernel(v_ref, stat_ref, gain_ref, offset_ref, m_ref, out_ref, t_ref):
    for x in range(8):
        for z in range(8):
            t_ref[pl.ds(64 * x + z, 8, stride=8), :] = v_ref[x, :, 128 * z : 128 * z + 128]
    value = scaled(t_ref[...], stat_ref, gain_ref, offset_ref)
    out_ref[0] = (value.T * m_ref[0]).astype(BF16)


def make_output(second, stat, gain, offset, mask_f):
    nb = mask_f.shape[0]
    row = pl.BlockSpec((1, 128), lambda b: (0, 0))
    return pl.pallas_call(
        final_kernel,
        grid=(nb,),
        out_shape=jax.ShapeDtypeStruct((nb, 128, 512), BF16),
        in_specs=[
            pl.BlockSpec((8, 8, 1024), lambda b: (0, b, 0)),
            pl.BlockSpec((8, 128), lambda b: (0, 0)),
            row,
            row,
            pl.BlockSpec((1, 1, 512), lambda b: (b, 0, 0)),
        ],
        out_specs=pl.BlockSpec((1, 128, 512), lambda b: (b, 0, 0)),
        scratch_shapes=[pltpu.VMEM((512, 128), F32)],
        compiler_params=params(32),
    )(second.reshape(8, nb * 8, 1024), stat, gain, offset, mask_f.reshape(nb, 1, 512))


def share(bundle, zface):
    face = bundle.shape[0] // 4
    count = lax.axis_size("corridor")
    forward = [(i, i + 1) for i in range(count - 1)]
    backward = [(target, source) for source, target in forward]
    before = lax.ppermute(bundle[face : 2 * face], "corridor", forward)
    after = lax.ppermute(bundle[0:face], "corridor", backward)
    zpool = lax.all_gather(zface, "group", axis=0, tiled=True)
    pool = lax.all_gather(
        jnp.concatenate([bundle, before, after], axis=0), "group", axis=0, tiled=True
    )
    return pool, zpool


def shards(
    features, voxel_mask, neighbours, weight_first, gain_first, offset_first,
    weight_second, gain_second, offset_second,
):
    nb = features.shape[0]
    face = nb * 8
    lanes = lax.axis_size("group")
    corridor_at = lax.axis_index("corridor")
    mask_f = voxel_mask.astype(F32)
    mask_rows = voxel_mask.astype(BF16).reshape(nb, 8, 8, 8).transpose(1, 0, 2, 3)
    mask_rows = jnp.pad(mask_rows.reshape(nb * 64, 8), ((0, 0), (0, 120)))

    safe = jnp.maximum(neighbours, 0)
    owner = safe // nb
    slot = safe % nb
    same = owner // lanes == corridor_at
    lane = owner % lanes
    dx = jnp.array([[step[0] for step in DIRECTIONS]], jnp.int32)
    dy = jnp.array([[step[1] for step in DIRECTIONS]], jnp.int32)
    x_part = jnp.where(dx < 0, jnp.where(same, 1, 4), jnp.where(same, 0, 5)) * face + slot * 8
    y_part = jnp.where(dy < 0, 3, 2) * face + slot
    place = lane * (6 * face) + jnp.where(dx != 0, x_part, y_part)
    z_only = (dx == 0) & (dy == 0)
    place = jnp.where(z_only, lane * (8 * face) + slot * 8, place)
    nothing = jnp.where(z_only, lanes * 8 * face, lanes * 6 * face)
    rows = jnp.where(neighbours >= 0, place, nothing).astype(jnp.int32)

    w1 = weight_first.transpose(0, 2, 1).reshape(9, 3, 64, 64)
    w1 = jnp.concatenate(
        [jnp.pad(w1, ((0, 0), (0, 1), (0, 0), (0, 0))), jnp.pad(w1, ((0, 0), (1, 0), (0, 0), (0, 0)))],
        axis=3,
    ).reshape(9 * 4 * 64, 128)
    w2 = weight_second.transpose(0, 2, 1).reshape(27 * 64, 128)
    gain1 = jnp.tile(gain_first, 2)[None]
    offset1 = jnp.tile(offset_first, 2)[None]

    field, bundle, zface = prepare(features, mask_f)
    pool, zpool = share(bundle, zface)
    first, stat = conv(rows, field, pool, zpool, w1, mask_rows, lanes, 64)
    stat = global_stats(stat, 1)
    field, bundle, zface = make_hidden(first, stat, gain1, offset1, mask_rows)
    pool, zpool = share(bundle, zface)
    second, stat = conv(rows, field, pool, zpool, w2, mask_rows, lanes, 128)
    stat = global_stats(stat, 1)
    return make_output(second, stat, gain_second[None], offset_second[None], mask_f)


def solution(mesh):
    in_specs = (
        P(("corridor", "group"), None, None),
        P(("corridor", "group"), None),
        P(("corridor", "group"), None),
        P(),
        P(),
        P(),
        P(),
        P(),
        P(),
    )
    out_specs = P(("corridor", "group"), None, None)
    return jax.shard_map(shards, mesh=mesh, in_specs=in_specs, out_specs=out_specs, check_vma=False)
```

```python
import functools

import jax
import jax.numpy as jnp
from jax import lax
from jax.experimental import pallas as pl
from jax.experimental.pallas import tpu as pltpu
from jax.sharding import PartitionSpec as P

DIRECTIONS = [
    (a, b, c) for a in (-1, 0, 1) for b in (-1, 0, 1) for c in (-1, 0, 1) if (a, b, c) != (0, 0, 0)
]
AT = {step: idx for idx, step in enumerate(DIRECTIONS)}
SOURCES = ((0, 1, 2, 3, 4, 5, 8, -1), (2, 3, 4, 5, 8, -1, 6, 7))
F32 = jnp.float32
BF16 = jnp.bfloat16
VMEM = pl.BlockSpec(memory_space=pltpu.VMEM)
SMEM = pl.BlockSpec(memory_space=pltpu.SMEM)
MESH = pl.DeviceIdType.MESH


def params(mib, **kw):
    return pltpu.CompilerParams(vmem_limit_bytes=mib * 1024 * 1024, **kw)


def spread(mask_rows, width):
    shift = {64: 6, 128: 7}[width]
    row = lax.broadcasted_iota(jnp.int32, (128, 8 * width), 0)
    lane = lax.broadcasted_iota(jnp.int32, (128, 8 * width), 1)
    pick = jnp.where((lane >> shift) == row, 1.0, 0.0).astype(BF16)
    return jnp.dot(mask_rows, pick, preferred_element_type=F32)


def emit_field(nb, tiles, field_ref, bundle_ref, z_ref):
    face = nb * 8
    for t in range(4):
        value = tiles[t]
        cols = slice(128 * t, 128 * t + 128)
        field_ref[:, cols] = value[...].astype(BF16)
        bundle_ref[0:face, cols] = value[0:face, :].astype(BF16)
        bundle_ref[face : 2 * face, cols] = value[7 * face : 8 * face, :].astype(BF16)
        bundle_ref[2 * face : 3 * face, cols] = value[pl.ds(0, face, stride=8), :].astype(BF16)
        bundle_ref[3 * face : 4 * face, cols] = value[pl.ds(7, face, stride=8), :].astype(BF16)
    lane = lax.broadcasted_iota(jnp.int32, (8 * face, 128), 1)
    z_ref[...] = jnp.where(lane < 64, tiles[0][...], tiles[3][...]).astype(BF16)


def field_shapes(nb):
    return (
        jax.ShapeDtypeStruct((nb * 64, 512), BF16),
        jax.ShapeDtypeStruct((nb * 32, 512), BF16),
        jax.ShapeDtypeStruct((nb * 64, 128), BF16),
    )


def prepare_kernel(nb, x_ref, m_ref, field_ref, bundle_ref, z_ref, t_ref, *tiles):
    lane = lax.broadcasted_iota(jnp.int32, (64, 128), 1)
    for pair in range(nb // 2):
        halves = [
            x_ref[2 * pair + k].astype(F32) * m_ref[pl.ds(2 * pair + k, 1), :] for k in range(2)
        ]
        t_ref[...] = jnp.concatenate(halves, axis=0).T
        for t in range(4):
            even = t_ref[pl.ds(2 * t, 64, stride=8), :]
            odd = t_ref[pl.ds(2 * t + 1, 64, stride=8), :]
            first = jnp.where(lane < 64, even, pltpu.roll(odd, 64, 1))
            second = jnp.where(lane < 64, pltpu.roll(even, 64, 1), odd)
            for x in range(8):
                base = x * nb * 8 + pair * 16
                tiles[t][base : base + 8, :] = first[8 * x : 8 * x + 8]
                tiles[t][base + 8 : base + 16, :] = second[8 * x : 8 * x + 8]
    emit_field(nb, tiles, field_ref, bundle_ref, z_ref)


def prepare(features, mask_f):
    nb = features.shape[0]
    return pl.pallas_call(
        functools.partial(prepare_kernel, nb),
        out_shape=field_shapes(nb),
        in_specs=[VMEM, VMEM],
        out_specs=(VMEM, VMEM, VMEM),
        scratch_shapes=[pltpu.VMEM((512, 128), F32)]
        + [pltpu.VMEM((nb * 64, 128), F32) for _ in range(4)],
        compiler_params=params(32),
    )(features, mask_f)


def conv_kernel(
    nb, lanes, outs, rows_ref, field_ref, pool_ref, zpool_ref, w_ref, m_ref,
    out_ref, stat_ref, own_ref, pf_ref, zf_ref, q_ref, wb_ref,
):
    face = nb * 8
    total = pool_ref.shape[0]
    ztotal = zpool_ref.shape[0]
    own_ref[...] = field_ref[...].astype(F32)
    pf_ref[0:total, :] = pool_ref[...].astype(F32)
    pf_ref[total:, :] = jnp.zeros((face, 512), F32)
    zf_ref[0:ztotal, :] = zpool_ref[...].astype(F32)
    zf_ref[ztotal:, :] = jnp.zeros((8 * face, 128), F32)

    wb_ref[...] = jnp.zeros(wb_ref.shape, BF16)
    for half in range(2):
        for a in range(3):
            for e in range(3):
                for at, source in enumerate(SOURCES[half]):
                    row = e * 512 + at * 64
                    for q in range(outs * 4 // 128):
                        z = 4 * half + q * 128 // outs
                        f = source - z + 1
                        kinds = 3 if outs == 128 else 4
                        if 0 <= f < kinds:
                            block = ((a * 3 + e) * kinds + f) * 64
                            wb_ref[half, a, row : row + 64, q * 128 : q * 128 + 128] = w_ref[
                                block : block + 64, :
                            ]

    low = lax.broadcasted_iota(jnp.int32, (8, 128), 1) < 64
    sub = lax.broadcasted_iota(jnp.int32, (8, 128), 0)

    def brick_planes(b):
        def at(dx, dy, dz):
            return rows_ref[b, AT[(dx, dy, dz)]]

        def faces(load):
            main = load(0)
            up = load(1)
            down = load(-1)
            tiles = [main[:, 128 * t : 128 * t + 128] for t in range(4)]
            width = main.shape[0]
            halo = jnp.where(low[:width], up[:, 0:128], down[:, 384:512])
            return [tiles[0], tiles[1], tiles[2], halo, tiles[3]]

        def x_face(dx, dy):
            def load(dz):
                return pf_ref[pl.ds(pl.multiple_of(at(dx, dy, dz), 8), 8), :]

            return faces(load)

        def y_row(dy, x):
            def load(dz):
                return pf_ref[pl.ds(at(0, dy, dz) + x * nb, 1), :]

            return [jnp.broadcast_to(v, (8, 128)) for v in faces(load)]

        def inner(x):
            base = pl.multiple_of(x * face + b * 8, 8)
            own = own_ref[pl.ds(base, 8), :]
            up = zf_ref[pl.ds(pl.multiple_of(at(0, 0, 1) + x * face, 8), 8), :]
            down = zf_ref[pl.ds(pl.multiple_of(at(0, 0, -1) + x * face, 8), 8), :]
            tiles = [own[:, 128 * t : 128 * t + 128] for t in range(4)]
            return [tiles[0], tiles[1], tiles[2], jnp.where(low, up, down), tiles[3]]

        planes = []
        for i in range(10):
            if i == 0 or i == 9:
                dx = -1 if i == 0 else 1
                centre = x_face(dx, 0)
                before = x_face(dx, -1)
                after = x_face(dx, 1)
            else:
                centre = inner(i - 1)
                before = y_row(-1, i - 1)
                after = y_row(1, i - 1)
            shifted0 = [
                pltpu.roll(jnp.where(sub == 7, n, c), 1, 0) for n, c in zip(before, centre)
            ]
            shifted2 = [
                pltpu.roll(jnp.where(sub == 0, n, c), 7, 0) for n, c in zip(after, centre)
            ]
            planes.append((shifted0, centre, shifted2))
        return planes

    @pl.loop(0, nb // 2)
    def _(pair):
        first = brick_planes(2 * pair)
        second = brick_planes(2 * pair + 1)
        for i in range(10):
            rows = pl.ds(pl.multiple_of(i * face + pair * 16, 16), 16)
            for e in range(3):
                tiles = [
                    jnp.concatenate([u, v], axis=0).astype(BF16)
                    for u, v in zip(first[i][e], second[i][e])
                ]
                for t in range(4):
                    q_ref[0, rows, e * 512 + t * 128 : e * 512 + t * 128 + 128] = tiles[t]
                    q_ref[1, rows, e * 512 + t * 128 : e * 512 + t * 128 + 128] = tiles[t + 1]

    mask_rows = m_ref[...]
    mask = spread(mask_rows, outs)
    sums = jnp.zeros((1, 128), F32)
    for half in range(2):
        acc = None
        for a in range(3):
            part = jnp.dot(
                q_ref[half, a * face : a * face + 8 * face, :],
                wb_ref[half, a],
                preferred_element_type=F32,
            )
            acc = part if acc is None else acc + part
        span = slice(half * 4 * outs, half * 4 * outs + 4 * outs)
        acc = acc * mask[:, span]
        out_ref[:, span] = acc
        column = jnp.sum(acc, axis=0, keepdims=True)
        for t in range(4 * outs // 128):
            sums = sums + column[:, 128 * t : 128 * t + 128]
    if outs == 64:
        sums = sums + pltpu.roll(sums, 64, 1)
    count = jnp.sum(mask_rows.astype(F32))
    mean = sums / jnp.maximum(count, 1.0)
    squares = jnp.zeros((1, 128), F32)
    for t in range(8 * outs // 128):
        span = slice(128 * t, 128 * t + 128)
        deviation = (out_ref[:, span] - mean) * mask[:, span]
        squares = squares + jnp.sum(deviation * deviation, axis=0, keepdims=True)
    if outs == 64:
        squares = squares + pltpu.roll(squares, 64, 1)
    stat_ref[...] = jnp.zeros((8, 128), F32)
    stat_ref[0:1, :] = sums
    stat_ref[1:2, :] = squares
    stat_ref[2:3, :] = jnp.full((1, 128), count, F32)


def conv(rows, field, pool, zpool, weight, mask_rows, lanes, outs):
    nb = rows.shape[0]
    return pl.pallas_call(
        functools.partial(conv_kernel, nb, lanes, outs),
        out_shape=(
            jax.ShapeDtypeStruct((nb * 64, 8 * outs), F32),
            jax.ShapeDtypeStruct((8, 128), F32),
        ),
        in_specs=[SMEM, VMEM, VMEM, VMEM, VMEM, VMEM],
        out_specs=(VMEM, VMEM),
        scratch_shapes=[
            pltpu.VMEM((nb * 64, 512), F32),
            pltpu.VMEM((pool.shape[0] + nb * 8, 512), F32),
            pltpu.VMEM((zpool.shape[0] + nb * 64, 128), F32),
            pltpu.VMEM((2, nb * 80, 1536), BF16),
            pltpu.VMEM((2, 3, 1536, 4 * outs), BF16),
        ],
        compiler_params=params(58),
    )(rows, field, pool, zpool, weight, mask_rows)


def merge(parts):
    sums = jnp.sum(parts[:, 0:1, :], axis=0)
    counts = jnp.sum(parts[:, 2:3, :], axis=0)
    mean = sums / jnp.maximum(counts, 1.0)
    gaps = parts[:, 0:1, :] / jnp.maximum(parts[:, 2:3, :], 1.0) - mean[None]
    squares = jnp.sum(parts[:, 1:2, :] + parts[:, 2:3, :] * gaps * gaps, axis=0)
    return sums, squares, counts


def stats_kernel(sections, lanes, stat_ref, out_ref, near, far, mid, send, recv, send2, recv2):
    s = lax.axis_index("corridor")
    g = lax.axis_index("group")
    barrier = pltpu.get_barrier_semaphore()

    def lane_peer(d):
        return (s, lax.rem(g + d, lanes))

    def section_peer(d):
        return (lax.rem(s + d, sections), g)

    @pl.loop(1, lanes)
    def _(d):
        pl.semaphore_signal(barrier, inc=1, device_id=lane_peer(d), device_id_type=MESH)

    @pl.loop(1, sections)
    def _(d):
        pl.semaphore_signal(barrier, inc=1, device_id=section_peer(d), device_id_type=MESH)

    pl.semaphore_wait(barrier, lanes + sections - 2)

    def exchange(src, dst, me, count, peer, send_sem, recv_sem):
        def copy(d, slot):
            return pltpu.make_async_remote_copy(
                src_ref=src, dst_ref=dst.at[slot], send_sem=send_sem.at[d],
                recv_sem=recv_sem.at[slot], device_id=peer(d), device_id_type=MESH,
            )

        @pl.loop(1, count)
        def _(d):
            copy(d, me).start()

        dst[me] = src[...]

        @pl.loop(1, count)
        def _(d):
            copy(d, lax.rem(me + count - d, count)).wait_recv()

        @pl.loop(1, count)
        def _(d):
            copy(d, me).wait_send()

    exchange(stat_ref, near, g, lanes, lane_peer, send, recv)
    sums, squares, counts = merge(near[...])
    mid[...] = jnp.zeros((8, 128), F32)
    mid[0:1, :] = sums
    mid[1:2, :] = squares
    mid[2:3, :] = counts
    exchange(mid, far, s, sections, section_peer, send2, recv2)
    sums, squares, counts = merge(far[...])
    out_ref[...] = jnp.zeros((8, 128), F32)
    out_ref[0:1, :] = sums / counts
    out_ref[1:2, :] = squares / counts


def global_stats(stat, collective):
    sections = lax.axis_size("corridor")
    lanes = lax.axis_size("group")
    return pl.pallas_call(
        functools.partial(stats_kernel, sections, lanes),
        out_shape=jax.ShapeDtypeStruct((8, 128), F32),
        in_specs=[VMEM],
        out_specs=VMEM,
        scratch_shapes=[
            pltpu.VMEM((lanes, 8, 128), F32),
            pltpu.VMEM((sections, 8, 128), F32),
            pltpu.VMEM((8, 128), F32),
            pltpu.SemaphoreType.DMA((lanes,)),
            pltpu.SemaphoreType.DMA((lanes,)),
            pltpu.SemaphoreType.DMA((sections,)),
            pltpu.SemaphoreType.DMA((sections,)),
        ],
        compiler_params=params(16, collective_id=collective, has_side_effects=True),
    )(stat)


def scaled(value, stat_ref, gain_ref, offset_ref):
    mean = stat_ref[0:1, :]
    deviation = value - mean
    root = jnp.sqrt(stat_ref[1:2, :] + 1e-05)
    return jnp.maximum(gain_ref[...] * deviation / root + offset_ref[...], 0.0)


def hidden_kernel(
    nb, v_ref, stat_ref, gain_ref, offset_ref, m_ref, field_ref, bundle_ref, z_ref, *tiles
):
    mask = spread(m_ref[...], 64)
    for t in range(4):
        span = slice(128 * t, 128 * t + 128)
        tiles[t][...] = scaled(v_ref[:, span], stat_ref, gain_ref, offset_ref) * mask[:, span]
    emit_field(nb, tiles, field_ref, bundle_ref, z_ref)


def make_hidden(first, stat, gain, offset, mask_rows):
    nb = first.shape[0] // 64
    return pl.pallas_call(
        functools.partial(hidden_kernel, nb),
        out_shape=field_shapes(nb),
        in_specs=[VMEM] * 5,
        out_specs=(VMEM, VMEM, VMEM),
        scratch_shapes=[pltpu.VMEM((nb * 64, 128), F32) for _ in range(4)],
        compiler_params=params(32),
    )(first, stat, gain, offset, mask_rows)


def final_kernel(v_ref, stat_ref, gain_ref, offset_ref, m_ref, out_ref, t_ref):
    for x in range(8):
        for z in range(8):
            t_ref[pl.ds(64 * x + z, 8, stride=8), :] = v_ref[x, :, 128 * z : 128 * z + 128]
    value = scaled(t_ref[...], stat_ref, gain_ref, offset_ref)
    out_ref[0] = (value.T * m_ref[0]).astype(BF16)


def make_output(second, stat, gain, offset, mask_f):
    nb = mask_f.shape[0]
    row = pl.BlockSpec((1, 128), lambda b: (0, 0))
    return pl.pallas_call(
        final_kernel,
        grid=(nb,),
        out_shape=jax.ShapeDtypeStruct((nb, 128, 512), BF16),
        in_specs=[
            pl.BlockSpec((8, 8, 1024), lambda b: (0, b, 0)),
            pl.BlockSpec((8, 128), lambda b: (0, 0)),
            row,
            row,
            pl.BlockSpec((1, 1, 512), lambda b: (b, 0, 0)),
        ],
        out_specs=pl.BlockSpec((1, 128, 512), lambda b: (b, 0, 0)),
        scratch_shapes=[pltpu.VMEM((512, 128), F32)],
        compiler_params=params(32),
    )(second.reshape(8, nb * 8, 1024), stat, gain, offset, mask_f.reshape(nb, 1, 512))


def halo_kernel(sections, lanes, face, bundle_ref, z_ref, pool_ref, zpool_ref, send, recv):
    s = lax.axis_index("corridor")
    g = lax.axis_index("group")
    half = lanes // 2
    other = g + 1 - 2 * lax.rem(g, 2)
    has = {2: s > 0, 3: s < sections - 1}
    far_lanes = [lax.rem(g + 2 * j, lanes) for j in range(1, half)]
    mirror = [lax.rem(other + 2 * j, lanes) for j in range(1, half)]

    def place(k, lane):
        if k == 1:
            return zpool_ref.at[pl.ds(pl.multiple_of(lane * (8 * face), 16), 8 * face), :]
        start, size = {0: (0, 4 * face), 2: (4 * face, face), 3: (5 * face, face)}[k]
        return pool_ref.at[pl.ds(pl.multiple_of(lane * (6 * face) + start, 16), size), :]

    def copy(k, lane, src, peer, slot):
        return pltpu.make_async_remote_copy(
            src_ref=src, dst_ref=place(k, lane), send_sem=send.at[slot],
            recv_sem=recv.at[k * lanes + lane], device_id=peer, device_id_type=MESH,
        )

    def across(k, j):
        src = {0: bundle_ref, 1: z_ref}.get(k)
        return copy(k, g, place(k, g) if src is None else src, (s, far_lanes[j]), j * 4 + k)

    def beside(k, j):
        lane = g if j == 0 else far_lanes[j - 1]
        src = {0: bundle_ref, 1: z_ref}.get(k) if j == 0 else None
        return copy(
            k, lane, place(k, lane) if src is None else src, (s, other), (half + j) * 4 + k
        )

    def arrive(k, lane):
        copy(k, lane, place(k, lane), (s, other), 0).wait_recv()

    def along(k):
        rows = pl.ds(face, face) if k == 2 else pl.ds(0, face)
        target = s + 1 if k == 2 else s - 1
        return copy(k, g, bundle_ref.at[rows, :], (target, g), 8 * half + k)

    def guarded(k, action):
        if k in has:
            pl.when(has[k])(action)
        else:
            action()

    barrier = pltpu.get_barrier_semaphore()

    def greet(peer):
        pl.semaphore_signal(barrier, inc=1, device_id=peer, device_id_type=MESH)

    greet((s, other))
    for lane in far_lanes:
        greet((s, lane))
    guarded(2, lambda: greet((s - 1, g)))
    guarded(3, lambda: greet((s + 1, g)))
    ends = jnp.where(s > 0, 1, 0) + jnp.where(s < sections - 1, 1, 0)
    pl.semaphore_wait(barrier, half + ends)

    guarded(3, lambda: along(2).start())
    guarded(2, lambda: along(3).start())
    for k in (0, 1):
        for j in range(half - 1):
            across(k, j).start()
    for k in (0, 1):
        beside(k, 0).start()
    pool_ref[pl.ds(pl.multiple_of(g * (6 * face), 16), 4 * face), :] = bundle_ref[...]
    zpool_ref[pl.ds(pl.multiple_of(g * (8 * face), 16), 8 * face), :] = z_ref[...]

    def pass_on(k):
        def action():
            arrive(k, g)
            for j in range(half - 1):
                across(k, j).start()
            beside(k, 0).start()

        return action

    def relay(k, j):
        def action():
            arrive(k, far_lanes[j])
            beside(k, j + 1).start()

        return action

    for k in (2, 3):
        guarded(k, pass_on(k))
    for k in range(4):
        for j in range(half - 1):
            guarded(k, relay(k, j))
    for k in range(4):
        for lane in [other] + mirror:
            guarded(k, lambda k=k, lane=lane: arrive(k, lane))
    guarded(3, lambda: along(2).wait_send())
    guarded(2, lambda: along(3).wait_send())
    for k in range(4):
        for j in range(half - 1):
            guarded(k, lambda k=k, j=j: across(k, j).wait_send())
        for j in range(half):
            guarded(k, lambda k=k, j=j: beside(k, j).wait_send())


def share(bundle, zface):
    face = bundle.shape[0] // 4
    sections = lax.axis_size("corridor")
    lanes = lax.axis_size("group")
    return pl.pallas_call(
        functools.partial(halo_kernel, sections, lanes, face),
        out_shape=(
            jax.ShapeDtypeStruct((lanes * 6 * face, 512), BF16),
            jax.ShapeDtypeStruct((lanes * 8 * face, 128), BF16),
        ),
        in_specs=[VMEM, VMEM],
        out_specs=(VMEM, VMEM),
        scratch_shapes=[
            pltpu.SemaphoreType.DMA((4 * lanes + 4,)),
            pltpu.SemaphoreType.DMA((4 * lanes,)),
        ],
        compiler_params=params(32, collective_id=2, has_side_effects=True),
    )(bundle, zface)


def shards(
    features, voxel_mask, neighbours, weight_first, gain_first, offset_first,
    weight_second, gain_second, offset_second,
):
    nb = features.shape[0]
    face = nb * 8
    lanes = lax.axis_size("group")
    corridor_at = lax.axis_index("corridor")
    mask_f = voxel_mask.astype(F32)
    mask_rows = voxel_mask.astype(BF16).reshape(nb, 8, 8, 8).transpose(1, 0, 2, 3)
    mask_rows = jnp.pad(mask_rows.reshape(nb * 64, 8), ((0, 0), (0, 120)))

    safe = jnp.maximum(neighbours, 0)
    owner = safe // nb
    slot = safe % nb
    same = owner // lanes == corridor_at
    lane = owner % lanes
    dx = jnp.array([[step[0] for step in DIRECTIONS]], jnp.int32)
    dy = jnp.array([[step[1] for step in DIRECTIONS]], jnp.int32)
    x_part = jnp.where(dx < 0, jnp.where(same, 1, 4), jnp.where(same, 0, 5)) * face + slot * 8
    y_part = jnp.where(dy < 0, 3, 2) * face + slot
    place = lane * (6 * face) + jnp.where(dx != 0, x_part, y_part)
    z_only = (dx == 0) & (dy == 0)
    place = jnp.where(z_only, lane * (8 * face) + slot * 8, place)
    nothing = jnp.where(z_only, lanes * 8 * face, lanes * 6 * face)
    rows = jnp.where(neighbours >= 0, place, nothing).astype(jnp.int32)

    w1 = weight_first.transpose(0, 2, 1).reshape(9, 3, 64, 64)
    w1 = jnp.concatenate(
        [jnp.pad(w1, ((0, 0), (0, 1), (0, 0), (0, 0))), jnp.pad(w1, ((0, 0), (1, 0), (0, 0), (0, 0)))],
        axis=3,
    ).reshape(9 * 4 * 64, 128)
    w2 = weight_second.transpose(0, 2, 1).reshape(27 * 64, 128)
    gain1 = jnp.tile(gain_first, 2)[None]
    offset1 = jnp.tile(offset_first, 2)[None]

    field, bundle, zface = prepare(features, mask_f)
    pool, zpool = share(bundle, zface)
    first, stat = conv(rows, field, pool, zpool, w1, mask_rows, lanes, 64)
    stat = global_stats(stat, 1)
    field, bundle, zface = make_hidden(first, stat, gain1, offset1, mask_rows)
    pool, zpool = share(bundle, zface)
    second, stat = conv(rows, field, pool, zpool, w2, mask_rows, lanes, 128)
    stat = global_stats(stat, 1)
    return make_output(second, stat, gain_second[None], offset_second[None], mask_f)


def solution(mesh):
    in_specs = (
        P(("corridor", "group"), None, None),
        P(("corridor", "group"), None),
        P(("corridor", "group"), None),
        P(),
        P(),
        P(),
        P(),
        P(),
        P(),
    )
    out_specs = P(("corridor", "group"), None, None)
    return jax.shard_map(shards, mesh=mesh, in_specs=in_specs, out_specs=out_specs, check_vma=False)
```
